32 devices in a mesh: groups: 2 (over y), space: 4 (over z), species: 2 (over x), sub: 2 (over core).
Axes of the slice: x: 2, y: 2, z: 4, core: 2. Of those that a mesh axis runs over, the one named last changes fastest.
Arguments:
- fields: bfloat16 [52, 128, 8, 128], P('species', ('groups', 'space'), 'sub'), parts along dimension 1, may hold values from -6 to 6
- targets: bfloat16 [96, 52, 2, 4, 128], P(('groups', 'space', 'sub'), 'species'), parts along dimension 0, may hold values from -6 to 6
- conv_weight: bfloat16 [52, 3, 3, 3, 52], P('species'), may hold values from -0.3125 to 0.3125
- group_map: int32 [52], replicated, may hold values from 0 to 3
- flame_ids: int32 [96], P(('groups', 'space', 'sub')), parts along dimension 0, may hold values from 0 to 7, as said below
- helpers: int32 [96, 1], P(('groups', 'space', 'sub')), parts along dimension 0, may hold values from 0 to 3; in each aligned block of 6 rows (0 to 5, 6 to 11, ...) at most 3 rows name the same one
Outputs:
- block_grad: bfloat16 [96, 52, 2, 4, 128], P(('groups', 'space', 'sub'), 'species'), parts along dimension 0
- helper_rates: bfloat16 [16, 52, 4, 3, 2, 4, 128], P(('groups', 'space', 'sub'), 'species'), parts along dimension 0
The draws below stay inside these ranges and needn't reach their ends.
There are 2 independent parts, one for each index of `groups`. The reference program is written for one: setup_inputs(seed, part) draws one part's arguments, and reference() takes and returns one part's arrays. A program takes and returns all parts, laid end to end along the dimension named above; an argument that names none is the same for every part. Nothing has to cross between parts.
Inputs may be any that keep to these rules, and one draw needn't show every extreme that they name: `flame_ids`: the 6 entries of one slab are different block numbers. `helpers`: among the 6 rows of one slab no helper is named more than 3 times; in some slabs one is named exactly 3 times.
All inputs are finite; a program needn't handle non-finite values.
Results may differ from the reference program's by a relative error of at most 0.0045.
Values may be sent and summed in bfloat16 or wider, within the bound.
A program may use at most 128 MiB of HBM per device.

```python
import math
import jax
import jax.numpy as jnp
import numpy as np
from jax import lax

S = 52
NGROUP = 4
BX = 2
CY = 4
CZ = 128
NB = 8
NF = 6
CAP = 3
SLABS = 8
NX = 64
NY = 8
N_SPACE = 4
N_SUB = 2


def draw_flame_ids(key, part):
    keys = jax.random.split(key, SLABS)

    def one_slab(single):
        return jax.random.permutation(single, NB)[:NF]
    chosen = jax.vmap(one_slab)(keys)
    return chosen.reshape(SLABS * NF).astype(jnp.int32)


def plant(result, own_key, low, high):
    index_at = [jax.random.randint(jax.random.fold_in(own_key, axis), (), 0, length) for axis, length in enumerate(result.shape)]
    longest = result.shape.index(max(result.shape))
    beside = index_at[:longest] + [(index_at[longest] + 1) % result.shape[longest]] + index_at[longest + 1:]
    return result.at[tuple(index_at)].set(low).at[tuple(beside)].set(high)


def block_levels(stream_key, shape, pieces, least, high):
    def one(axis_at, blocks):
        heights = jax.random.uniform(jax.random.fold_in(jax.random.fold_in(stream_key, 6), axis_at), (blocks,), jnp.float32, least / len(pieces), high / len(pieces))
        return jnp.repeat(jnp.exp(heights), shape[axis_at] // blocks).reshape((-1,) + (1,) * (len(shape) - axis_at - 1))

    loudness = one(*pieces[0])
    for cut in pieces[1:]:
        loudness = loudness * one(*cut)
    return loudness


def routed_block(rng, own, number, rows, number_of, top, reach, skew):
    sequence = jax.random.permutation(rng, number_of)
    packed, common = portions_of(number_of, rows * top, reach, skew, True), portions_of(number_of, rows * top, reach, skew, False)
    places = jnp.arange(number_of)

    def named(lengths, turn):
        used = int((lengths > 0).sum())
        fixed = max(1, used // 4)
        shifted = fixed + (places - fixed + turn * (used - fixed)) % max(1, number_of - fixed)
        return jnp.zeros((number_of,), jnp.int32).at[sequence[jnp.where(places < fixed, places, shifted)]].set(jnp.asarray(lengths, jnp.int32))

    lengths = jnp.where(number % 4 == 0, named(packed, number // 4), named(common, number - number // 4 - 1))
    mixed = jax.random.permutation(jax.random.fold_in(own, 3), number_of)
    source_of, taker = mixed[0:number_of // 2 * 2:2], mixed[1:number_of // 2 * 2:2]
    margin = jnp.minimum(lengths[source_of] - 1, reach - lengths[taker]) // 2
    margin = jnp.where((source_of == sequence[0]) | (taker == sequence[0]) | (lengths[taker] == 0), 0, jnp.maximum(margin, 0))
    shifted = jax.random.randint(jax.random.fold_in(own, 4), (number_of // 2,), 0, 1 << 20) % (margin + 1)
    lengths = lengths.at[source_of].add(-shifted).at[taker].add(shifted)
    items = jnp.searchsorted(jnp.cumsum(lengths), jnp.arange(rows * top), side="right").astype(jnp.int32)
    grid = items.reshape(top, rows).T
    grid = grid[jax.random.permutation(jax.random.fold_in(own, 1), rows)]
    turn = jax.random.randint(jax.random.fold_in(own, 2), (rows, 1), 0, top)
    return jnp.take_along_axis(grid, (jnp.arange(top)[None, :] + turn) % top, axis=1)


def portions_of(count, total, reach, skew, full):
    portions = [(1 << 20) // math.isqrt(rank ** skew) + 1 for rank in range(1, count + 1)]
    largest = reach if full else min(reach, max(-(-total // count), total * portions[0] // sum(portions)))
    least = 1 if total - largest >= count - 1 else 0
    given, rest = [largest] + [least] * (count - 1), total - largest - least * (count - 1)
    while rest > 0:
        candidates = [i for i in range(1, count) if given[i] < largest] or [i for i in range(1, count) if given[i] < reach]
        whole, left = sum([portions[i] for i in candidates]), rest
        for i in candidates:
            extra = min(reach - given[i], max(1, left * portions[i] // whole), rest)
            given[i] = given[i] + extra
            rest = rest - extra
    return np.array(given)


def noise(key, extent, deviation, reach, cuts=(), kind=jnp.bfloat16):
    drawn = deviation * jax.random.normal(key, extent, jnp.float32)
    if cuts:
        drawn = drawn * block_levels(key, extent, cuts, -0.22, 0.18)
    return jnp.clip(drawn, -reach, reach).astype(kind)


def setup_inputs(seed: int = 0, part: int = 0) -> dict:
    key_of = jax.random.split(jax.random.key(seed), 7)
    own_keys = jax.random.split(jax.random.fold_in(key_of[6], part), 7)
    fields = noise(own_keys[0], (S, NX, NY, CZ), 1.0, 6.0, ((0, 2), (1, 4), (2, 2)))
    targets = noise(own_keys[1], (SLABS * NF, S, BX, CY, CZ), 1.0, 6.0, ((0, 8), (1, 2)))
    conv_weight = noise(key_of[2], (S, 3, 3, 3, S), (27 * S // NGROUP) ** -0.5, 0.3125, ((0, 2),))
    group_map = plant(jax.random.randint(key_of[3], (S,), 0, NGROUP), jax.random.fold_in(key_of[3], 1), 0, NGROUP - 1).astype(jnp.int32)
    flame_ids = draw_flame_ids(jax.random.fold_in(jax.random.fold_in(key_of[6], part), 71), part)
    helpers_keys = jax.random.split(jax.random.fold_in(own_keys[5], 1), (SLABS * NF) // NF)
    helpers_turns = jax.random.permutation(jax.random.fold_in(own_keys[5], 3), (SLABS * NF) // NF)
    helpers = jax.vmap(lambda own, number: routed_block(jax.random.fold_in(own_keys[5], 2), own, number, NF, N_SPACE, 1, CAP, 2))(helpers_keys, helpers_turns).reshape((SLABS * NF, 1))
    return {"fields": fields, "targets": targets, "conv_weight": conv_weight, "group_map": group_map, "flame_ids": flame_ids, "helpers": helpers}


def convolve(inputs, kernel):
    return lax.conv_general_dilated(inputs, kernel, (1, 1, 1), ((0, 0), (0, 0), (1, 1)), dimension_numbers=("NCDHW", "OIDHW", "NCDHW"), precision=lax.Precision.HIGHEST)


def reference(fields, targets, conv_weight, group_map, flame_ids, helpers):
    same_group = (group_map[:, None] == group_map[None, :]).astype(jnp.float32)
    weights = conv_weight.astype(jnp.float32) * same_group[:, None, None, None, :]
    forward = jnp.transpose(weights, (0, 4, 1, 2, 3))
    backward = jnp.transpose(jnp.flip(weights, (1, 2, 3)), (4, 0, 1, 2, 3))
    padded = jnp.pad(fields, ((0, 0), (1, 1), (1, 1), (0, 0)))
    slab_ids = jnp.arange(SLABS, dtype=jnp.int32)
    first_x = (slab_ids // N_SUB) * (NB * BX)
    first_y = (slab_ids % N_SUB) * CY
    block_ids = flame_ids.reshape(SLABS, NF)
    target_blocks = targets.reshape(SLABS, NF, S, BX, CY, CZ)

    def per_slab(inputs):
        x_start, y_start, chosen, wanted = inputs

        def cut_block(block_id):
            zero = jnp.zeros((), jnp.int32)
            return lax.dynamic_slice(padded, (zero, x_start + block_id * BX, y_start, zero), (S, BX + 2, CY + 2, CZ))

        patches = jax.vmap(cut_block)(chosen).astype(jnp.float32)
        predicted = convolve(patches, forward)
        misfit = (predicted - wanted.astype(jnp.float32)).astype(jnp.bfloat16)
        misfit = lax.optimization_barrier(misfit).astype(jnp.float32)
        misfit = jnp.pad(misfit, ((0, 0), (0, 0), (1, 1), (1, 1), (0, 0)))
        grads = convolve(misfit, backward)
        return grads.astype(jnp.bfloat16), predicted.astype(jnp.bfloat16)

    grads, rates = lax.map(per_slab, (first_x, first_y, block_ids, target_blocks))
    block_grad = grads.reshape(SLABS * NF, S, BX, CY, CZ)
    helper_of = helpers[:, 0].reshape(SLABS, NF)
    order = jnp.arange(NF, dtype=jnp.int32)
    earlier = (helper_of[:, None, :] == helper_of[:, :, None]) & (order[None, None, :] < order[None, :, None])
    slot_rank = jnp.sum(earlier.astype(jnp.int32), axis=2)
    target_slab = helper_of * N_SUB + (slab_ids % N_SUB)[:, None]
    source = jnp.broadcast_to((slab_ids // N_SUB)[:, None], (SLABS, NF))
    helper_rates = jnp.zeros((SLABS, S, N_SPACE, CAP, BX, CY, CZ), jnp.bfloat16)
    helper_rates = helper_rates.at[target_slab, :, source, slot_rank].set(rates)
    return block_grad, helper_rates
```

```python
import jax
import jax.numpy as jnp
from jax import lax
from jax.sharding import PartitionSpec as P


def extended(value, sides, width):
    for axis, dim in sides:
        size, length = (lax.axis_size(axis), value.shape[dim])
        up = [(i, (i + 1) % size) for i in range(size - 1)]
        down = [(j, i) for i, j in up]
        last = lax.slice_in_dim(value, length - width, length, axis=dim)
        first = lax.slice_in_dim(value, 0, width, axis=dim)
        before = lax.ppermute(last, axis, up)
        after = lax.ppermute(first, axis, down)
        value = jnp.concatenate([before, value, after], axis=dim)
    return value


def tiles_from(pieces):
    count = len(pieces)
    got = [pieces[0]]
    for d in range(1, count):
        pairs = [(j, (j - d) % count) for j in range(count)]
        got.append(lax.ppermute(pieces[d], "species", pairs))
    return got


def convolve(inputs, kernel):
    return lax.conv_general_dilated(
        inputs,
        kernel,
        (1, 1, 1),
        ((0, 0), (0, 0), (1, 1)),
        dimension_numbers=("CNDHW", "OIDHW", "CNDHW"),
        preferred_element_type=jnp.float32,
    )


def shards(fields, targets, conv_weight, group_map, flame_ids, helpers):
    width = fields.shape[0]
    block_len = targets.shape[2]
    cells = targets.shape[2:]
    flames = flame_ids.shape[0]
    nspace = lax.axis_size("space")
    capacity = max(2, 2 * flames // nspace)
    tile = lax.axis_index("species")
    count = lax.axis_size("species")

    def columns(step):
        start = (tile + step) % count * width
        return lax.dynamic_slice_in_dim(conv_weight, start, width, 4)

    maps = [lax.dynamic_slice_in_dim(group_map, (tile + d) % count * width, width) for d in range(count)]
    same = (maps[0][:, None] == jnp.concatenate(maps)[None, :]).astype(jnp.bfloat16)
    rows = tiles_from([columns(count - d if d else 0) for d in range(count)])
    w_fwd = jnp.concatenate([columns(d) for d in range(count)], 4) * same[:, None, None, None, :]
    w_bwd = jnp.concatenate(rows, 0) * same.T[:, None, None, None, :]
    padded = extended(fields, (("space", 1), ("sub", 2)), 1)
    padded = jnp.concatenate(tiles_from([padded] * count), 0)

    def cut_block(block_id):
        return lax.dynamic_slice_in_dim(padded, block_id * block_len, block_len + 2, 1)

    patches = jnp.stack([cut_block(flame_ids[j]) for j in range(flames)], 1)
    predicted = convolve(patches, jnp.transpose(w_fwd, (0, 4, 1, 2, 3)))
    wanted = jnp.transpose(targets, (1, 0, 2, 3, 4)).astype(jnp.float32)
    misfit = (predicted - wanted).astype(jnp.bfloat16)
    misfit = jnp.concatenate(tiles_from([misfit] * count), 0)
    misfit = jnp.pad(misfit, ((0, 0), (0, 0), (1, 1), (1, 1), (0, 0)))
    kernel = jnp.transpose(jnp.flip(w_bwd, (1, 2, 3)), (4, 0, 1, 2, 3))
    grads = convolve(misfit, kernel).astype(jnp.bfloat16)
    block_grad = jnp.transpose(grads, (1, 0, 2, 3, 4))

    helper_of = helpers[:, 0]
    order = jnp.arange(flames)
    earlier = (helper_of[None, :] == helper_of[:, None]) & (order[None, :] < order[:, None])
    slot_rank = jnp.sum(earlier.astype(jnp.int32), axis=1)
    slot_index = helper_of * capacity + slot_rank
    onehot = (jnp.arange(nspace * capacity)[:, None] == slot_index[None, :]).astype(jnp.bfloat16)
    slots = jnp.einsum(
        "kj,cjxyz->ckxyz", onehot, predicted.astype(jnp.bfloat16), preferred_element_type=jnp.float32
    ).astype(jnp.bfloat16)
    slots = slots.reshape((width, nspace, capacity) + cells)
    rates = lax.all_to_all(slots, "space", split_axis=1, concat_axis=1, tiled=True)
    return (block_grad, rates[None])


def solution(mesh):
    placed = (
        P("species", ("groups", "space"), "sub", None),
        P(("groups", "space", "sub"), "species", None, None, None),
        P("species", None, None, None, None),
        P(),
        P(("groups", "space", "sub")),
        P(("groups", "space", "sub"), None),
    )
    return jax.shard_map(
        shards,
        mesh=mesh,
        in_specs=placed,
        out_specs=(
            P(("groups", "space", "sub"), "species", None, None, None),
            P(("groups", "space", "sub"), "species", None, None, None, None, None),
        ),
        check_vma=False,
    )
```

```python
import functools
import jax
import jax.numpy as jnp
from jax import lax
from jax.experimental import pallas as pl
from jax.experimental.pallas import tpu as pltpu
from jax.sharding import PartitionSpec as P


def space_halo(fields):
    size = lax.axis_size("space")
    up = [(i, i + 1) for i in range(size - 1)]
    down = [(j, i) for i, j in up]
    before = lax.ppermute(fields[:, -1:], "space", up)
    after = lax.ppermute(fields[:, :1], "space", down)
    return before, after


def tiles_from(pieces):
    count = len(pieces)
    got = [pieces[0]]
    for d in range(1, count):
        pairs = [(j, (j - d) % count) for j in range(count)]
        got.append(lax.ppermute(pieces[d], "species", pairs))
    return got


def edges_from(edge, count):
    got = []
    for d in range(count):
        pairs = [(j * 2 + s, (j - d) % count * 2 + 1 - s) for j in range(count) for s in range(2)]
        got.append(lax.ppermute(edge, ("species", "sub"), pairs))
    return got


def channel_rows(value, padded):
    c, x, y, z = value.shape
    rows = jnp.transpose(value, (1, 0, 2, 3)).reshape(x, c, y * z)
    return jnp.pad(rows, ((0, 0), (0, padded - c), (0, 0)))


def packed_weight(pieces, padded):
    w = jnp.stack(pieces, 0)
    t, r, _, _, _, k = w.shape
    w = jnp.pad(w, ((0, 0), (0, padded - r), (0, 0), (0, 0), (0, 0), (0, padded - k)))
    w = jnp.transpose(w, (4, 1, 2, 3, 0, 5))
    return w.reshape(3 * padded, 9 * t * padded)


def shifted_sum(product, rows, z):
    lanes = product.shape[1]
    at = lax.broadcasted_iota(jnp.int32, (rows, lanes), 1) % z
    low = pltpu.roll(product[:rows], 1, 1)
    high = pltpu.roll(product[2 * rows :], lanes - 1, 1)
    return product[rows : 2 * rows] + jnp.where(at == 0, 0.0, low) + jnp.where(at == z - 1, 0.0, high)


def forward(count, z, ids, slot, *refs):
    mains, befores, afters = refs[:count], refs[count : 2 * count], refs[2 * count : 3 * count]
    w, wanted, misfit, slots, stack = refs[3 * count :]
    flames, length, rows, lanes = wanted.shape
    slots[...] = jnp.zeros_like(slots)
    for j in range(flames):
        first = ids[j] * length
        buf = stack.at[j % 2]
        for u in range(length):
            o = u * lanes
            for a in range(3):
                for t in range(count):
                    k = [pl.ds(((a * 3 + b) * count + t) * rows, rows) for b in range(3)]
                    main = mains[t][first + u + a]
                    buf[k[0], o : o + z] = befores[t][first + u + a]
                    buf[k[0], o + z : o + lanes] = main[:, : lanes - z]
                    buf[k[1], o : o + lanes] = main
                    buf[k[2], o : o + lanes - z] = main[:, z:]
                    buf[k[2], o + lanes - z : o + lanes] = afters[t][first + u + a]
        product = jnp.dot(w[...], buf[...], preferred_element_type=jnp.float32)
        total = shifted_sum(product, rows, z)
        place = slot[j]
        for u in range(length):
            part = total[:, u * lanes : (u + 1) * lanes]
            slots[place, u] = part.astype(slots.dtype)
            misfit[j, u] = (part - wanted[j, u].astype(jnp.float32)).astype(misfit.dtype)


def backward(count, z, *refs):
    misfits = refs[:count]
    w, grads, stack = refs[count:]
    flames, length, rows, lanes = grads.shape
    stack[...] = jnp.zeros_like(stack)
    for j in range(flames):
        buf = stack.at[j % 2]
        for u in range(length):
            o = u * lanes
            for a in range(3):
                x = u + 1 - a
                if x < 0 or x >= length:
                    continue
                for t in range(count):
                    k = [pl.ds(((a * 3 + b) * count + t) * rows, rows) for b in range(3)]
                    part = misfits[t][j, x]
                    buf[k[0], o : o + lanes - z] = part[:, z:]
                    buf[k[1], o : o + lanes] = part
                    buf[k[2], o + z : o + lanes] = part[:, : lanes - z]
        product = jnp.dot(w[...], buf[...], preferred_element_type=jnp.float32)
        total = shifted_sum(product, rows, z)
        for u in range(length):
            grads[j, u] = total[:, u * lanes : (u + 1) * lanes].astype(grads.dtype)


def shards(fields, targets, conv_weight, group_map, flame_ids, helpers):
    width = fields.shape[0]
    flames = flame_ids.shape[0]
    length, ny, nz = targets.shape[2:]
    lanes = ny * nz
    padded = -(-width // 16) * 16
    nspace = lax.axis_size("space")
    count = lax.axis_size("species")
    capacity = max(2, 2 * flames // nspace)
    tile = lax.axis_index("species")
    sub = lax.axis_index("sub")

    x_before, x_after = space_halo(fields)
    main = jnp.concatenate(
        [channel_rows(x_before, padded), channel_rows(fields, padded), channel_rows(x_after, padded)], 0
    )
    mains = tiles_from([main] * count)
    edge = jnp.where(sub == 0, main[:, :, lanes - nz :], main[:, :, :nz])
    edges = edges_from(edge, count)
    zero = jnp.zeros_like(edge)
    befores = [jnp.where(sub == 1, e, zero) for e in edges]
    afters = [jnp.where(sub == 0, e, zero) for e in edges]

    def columns(step):
        start = (tile + step) % count * width
        return lax.dynamic_slice_in_dim(conv_weight, start, width, 4)

    maps = [lax.dynamic_slice_in_dim(group_map, (tile + d) % count * width, width) for d in range(count)]
    same = [(maps[0][:, None] == m[None, :]).astype(jnp.bfloat16) for m in maps]
    rows = tiles_from([columns(count - d if d else 0) for d in range(count)])
    w_fwd = packed_weight([columns(d) * same[d][:, None, None, None, :] for d in range(count)], padded)
    w_bwd = packed_weight(
        [
            jnp.transpose(jnp.flip(rows[d], 3) * same[d].T[:, None, None, None, :], (4, 1, 2, 3, 0))
            for d in range(count)
        ],
        padded,
    )

    wanted = jnp.transpose(targets, (0, 2, 1, 3, 4)).reshape(flames, length, width, lanes)
    wanted = jnp.pad(wanted, ((0, 0), (0, 0), (0, padded - width), (0, 0)))
    helper_of = helpers[:, 0]
    order = jnp.arange(flames)
    earlier = (helper_of[None, :] == helper_of[:, None]) & (order[None, :] < order[:, None])
    slot_index = helper_of * capacity + jnp.sum(earlier.astype(jnp.int32), axis=1)

    vmem = pl.BlockSpec(memory_space=pltpu.VMEM)
    smem = pl.BlockSpec(memory_space=pltpu.SMEM)
    params = pltpu.CompilerParams(vmem_limit_bytes=32 * 1024 * 1024)
    stack = pltpu.VMEM((2, 9 * count * padded, length * lanes), jnp.bfloat16)
    flops = 2 * flames * w_fwd.size * length * lanes
    cost = pl.CostEstimate(flops=flops, bytes_accessed=4_000_000, transcendentals=0)
    misfit, slots = pl.pallas_call(
        functools.partial(forward, count, nz),
        out_shape=(
            jax.ShapeDtypeStruct((flames, length, padded, lanes), jnp.bfloat16),
            jax.ShapeDtypeStruct((nspace * capacity, length, padded, lanes), jnp.bfloat16),
        ),
        in_specs=[smem, smem] + [vmem] * (3 * count + 2),
        out_specs=(vmem, vmem),
        scratch_shapes=[stack],
        compiler_params=params,
        cost_estimate=cost,
    )(flame_ids, slot_index, *mains, *befores, *afters, w_fwd, wanted)
    misfits = tiles_from([misfit] * count)
    slots = slots.reshape(nspace, capacity, length, padded, lanes)
    rates = lax.all_to_all(slots, "space", split_axis=0, concat_axis=0, tiled=True)
    grads = pl.pallas_call(
        functools.partial(backward, count, nz),
        out_shape=jax.ShapeDtypeStruct((flames, length, padded, lanes), jnp.bfloat16),
        in_specs=[vmem] * (count + 1),
        out_specs=vmem,
        scratch_shapes=[stack],
        compiler_params=params,
        cost_estimate=cost,
    )(*misfits, w_bwd)
    grads = grads[:, :, :width].reshape(flames, length, width, ny, nz)
    block_grad = jnp.transpose(grads, (0, 2, 1, 3, 4))
    rates = rates[:, :, :, :width].reshape(nspace, capacity, length, width, ny, nz)
    return (block_grad, jnp.transpose(rates, (3, 0, 1, 2, 4, 5))[None])


def solution(mesh):
    placed = (
        P("species", ("groups", "space"), "sub", None),
        P(("groups", "space", "sub"), "species", None, None, None),
        P("species", None, None, None, None),
        P(),
        P(("groups", "space", "sub")),
        P(("groups", "space", "sub"), None),
    )
    return jax.shard_map(
        shards,
        mesh=mesh,
        in_specs=placed,
        out_specs=(
            P(("groups", "space", "sub"), "species", None, None, None),
            P(("groups", "space", "sub"), "species", None, None, None, None, None),
        ),
        check_vma=False,
    )
```

```python
import functools
import jax
import jax.numpy as jnp
from jax import lax
from jax.experimental import pallas as pl
from jax.experimental.pallas import tpu as pltpu
from jax.sharding import PartitionSpec as P


def space_halo(fields):
    size = lax.axis_size("space")
    up = [(i, i + 1) for i in range(size - 1)]
    down = [(j, i) for i, j in up]
    before = lax.ppermute(fields[:, -1:], "space", up)
    after = lax.ppermute(fields[:, :1], "space", down)
    return before, after


def tiles_from(pieces):
    count = len(pieces)
    got = [pieces[0]]
    for d in range(1, count):
        pairs = [(j, (j - d) % count) for j in range(count)]
        got.append(lax.ppermute(pieces[d], "species", pairs))
    return got


def edges_from(edge, count):
    got = []
    for d in range(count):
        pairs = [(j * 2 + s, (j - d) % count * 2 + 1 - s) for j in range(count) for s in range(2)]
        got.append(lax.ppermute(edge, ("species", "sub"), pairs))
    return got


def rates_from(slots):
    size, me = lax.axis_size("space"), lax.axis_index("space")
    got = [lax.dynamic_index_in_dim(slots, me, 0, keepdims=False)]
    for d in range(1, size):
        piece = lax.dynamic_index_in_dim(slots, (me + d) % size, 0, keepdims=False)
        got.append(lax.ppermute(piece, "space", [(j, (j + d) % size) for j in range(size)]))
    turned = jnp.stack(got[::-1], 0)
    start = (size - 1 - me) % size
    return lax.dynamic_slice_in_dim(jnp.concatenate([turned, turned], 0), start, size, 0)


def channel_rows(value, padded):
    c, x, y, z = value.shape
    rows = jnp.transpose(value, (1, 0, 2, 3)).reshape(x, c, y * z)
    return jnp.pad(rows, ((0, 0), (0, padded - c), (0, 0)))


def packed_weight(pieces, padded):
    w = jnp.stack(pieces, 0)
    t, r, _, _, _, k = w.shape
    w = jnp.pad(w, ((0, 0), (0, padded - r), (0, 0), (0, 0), (0, 0), (0, padded - k)))
    w = jnp.transpose(w, (4, 1, 2, 3, 0, 5))
    return w.reshape(3 * padded, 9 * t * padded)


def shifted_sum(product, rows, z):
    lanes = product.shape[1]
    at = lax.broadcasted_iota(jnp.int32, (rows, lanes), 1) % z
    low = pltpu.roll(product[:rows], 1, 1)
    high = pltpu.roll(product[2 * rows :], lanes - 1, 1)
    return product[rows : 2 * rows] + jnp.where(at == 0, 0.0, low) + jnp.where(at == z - 1, 0.0, high)


def forward(count, z, ids, slot, *refs):
    mains, befores, afters = refs[:count], refs[count : 2 * count], refs[2 * count : 3 * count]
    w, wanted, misfit, slots, stack = refs[3 * count :]
    flames, length, rows, lanes = wanted.shape
    slots[...] = jnp.zeros_like(slots)
    for j in range(flames):
        first = ids[j] * length
        buf = stack.at[j % 2]
        for u in range(length):
            o = u * lanes
            for a in range(3):
                for t in range(count):
                    k = [pl.ds(((a * 3 + b) * count + t) * rows, rows) for b in range(3)]
                    main = mains[t][first + u + a]
                    buf[k[0], o : o + z] = befores[t][first + u + a]
                    buf[k[0], o + z : o + lanes] = main[:, : lanes - z]
                    buf[k[1], o : o + lanes] = main
                    buf[k[2], o : o + lanes - z] = main[:, z:]
                    buf[k[2], o + lanes - z : o + lanes] = afters[t][first + u + a]
        product = jnp.dot(w[...], buf[...], preferred_element_type=jnp.float32)
        total = shifted_sum(product, rows, z)
        place = slot[j]
        for u in range(length):
            part = total[:, u * lanes : (u + 1) * lanes]
            slots[place, u] = part.astype(slots.dtype)
            misfit[j, u] = (part - wanted[j, u].astype(jnp.float32)).astype(misfit.dtype)


def backward(count, z, *refs):
    misfits = refs[:count]
    w, grads, stack = refs[count:]
    flames, length, rows, lanes = grads.shape
    stack[...] = jnp.zeros_like(stack)
    for j in range(flames):
        buf = stack.at[j % 2]
        for u in range(length):
            o = u * lanes
            for a in range(3):
                x = u + 1 - a
                if x < 0 or x >= length:
                    continue
                for t in range(count):
                    k = [pl.ds(((a * 3 + b) * count + t) * rows, rows) for b in range(3)]
                    part = misfits[t][j, x]
                    buf[k[0], o : o + lanes - z] = part[:, z:]
                    buf[k[1], o : o + lanes] = part
                    buf[k[2], o + z : o + lanes] = part[:, : lanes - z]
        product = jnp.dot(w[...], buf[...], preferred_element_type=jnp.float32)
        total = shifted_sum(product, rows, z)
        for u in range(length):
            grads[j, u] = total[:, u * lanes : (u + 1) * lanes].astype(grads.dtype)


def shards(fields, targets, conv_weight, group_map, flame_ids, helpers):
    width = fields.shape[0]
    flames = flame_ids.shape[0]
    length, ny, nz = targets.shape[2:]
    lanes = ny * nz
    padded = -(-width // 16) * 16
    nspace = lax.axis_size("space")
    count = lax.axis_size("species")
    capacity = max(2, 2 * flames // nspace)
    tile = lax.axis_index("species")
    sub = lax.axis_index("sub")

    raw = tiles_from([fields] * count)
    raw_edges = edges_from(jnp.where(sub == 0, fields[:, :, -1], fields[:, :, 0]), count)
    halo = jnp.concatenate(space_halo(fields), 1)
    halos = tiles_from([halo] * count)
    halo_edges = edges_from(jnp.where(sub == 0, halo[:, :, -1], halo[:, :, 0]), count)

    def with_halo(inner, outer):
        return jnp.concatenate([outer[:, :1], inner, outer[:, 1:]], 1)

    mains = [channel_rows(with_halo(r, h), padded) for r, h in zip(raw, halos)]
    edges = [channel_rows(with_halo(r, h)[:, :, None], padded) for r, h in zip(raw_edges, halo_edges)]
    befores = [jnp.where(sub == 1, e, jnp.zeros_like(e)) for e in edges]
    afters = [jnp.where(sub == 0, e, jnp.zeros_like(e)) for e in edges]

    def columns(step):
        start = (tile + step) % count * width
        return lax.dynamic_slice_in_dim(conv_weight, start, width, 4)

    maps = [lax.dynamic_slice_in_dim(group_map, (tile + d) % count * width, width) for d in range(count)]
    same = [(maps[0][:, None] == m[None, :]).astype(jnp.bfloat16) for m in maps]
    rows = tiles_from([columns(count - d if d else 0) for d in range(count)])
    w_fwd = packed_weight([columns(d) * same[d][:, None, None, None, :] for d in range(count)], padded)
    w_bwd = packed_weight(
        [
            jnp.transpose(jnp.flip(rows[d], 3) * same[d].T[:, None, None, None, :], (4, 1, 2, 3, 0))
            for d in range(count)
        ],
        padded,
    )

    w_fwd, w_bwd = lax.optimization_barrier((w_fwd, w_bwd))

    wanted = jnp.transpose(targets, (0, 2, 1, 3, 4)).reshape(flames, length, width, lanes)
    wanted = jnp.pad(wanted, ((0, 0), (0, 0), (0, padded - width), (0, 0)))
    helper_of = helpers[:, 0]
    order = jnp.arange(flames)
    earlier = (helper_of[None, :] == helper_of[:, None]) & (order[None, :] < order[:, None])
    slot_index = helper_of * capacity + jnp.sum(earlier.astype(jnp.int32), axis=1)

    vmem = pl.BlockSpec(memory_space=pltpu.VMEM)
    smem = pl.BlockSpec(memory_space=pltpu.SMEM)
    params = pltpu.CompilerParams(vmem_limit_bytes=32 * 1024 * 1024)
    stack = pltpu.VMEM((2, 9 * count * padded, length * lanes), jnp.bfloat16)
    flops = 2 * flames * w_fwd.size * length * lanes
    cost = pl.CostEstimate(flops=flops, bytes_accessed=4_000_000, transcendentals=0)
    misfit, slots = pl.pallas_call(
        functools.partial(forward, count, nz),
        out_shape=(
            jax.ShapeDtypeStruct((flames, length, padded, lanes), jnp.bfloat16),
            jax.ShapeDtypeStruct((nspace * capacity, length, padded, lanes), jnp.bfloat16),
        ),
        in_specs=[smem, smem] + [vmem] * (3 * count + 2),
        out_specs=(vmem, vmem),
        scratch_shapes=[stack],
        compiler_params=params,
        cost_estimate=cost,
    )(flame_ids, slot_index, *mains, *befores, *afters, w_fwd, wanted)
    misfits = tiles_from([misfit] * count)
    slots = slots.reshape(nspace, capacity, length, padded, lanes)
    rates = rates_from(slots)
    grads = pl.pallas_call(
        functools.partial(backward, count, nz),
        out_shape=jax.ShapeDtypeStruct((flames, length, padded, lanes), jnp.bfloat16),
        in_specs=[vmem] * (count + 1),
        out_specs=vmem,
        scratch_shapes=[stack],
        compiler_params=params,
        cost_estimate=cost,
    )(*misfits, w_bwd)
    grads = grads[:, :, :width].reshape(flames, length, width, ny, nz)
    block_grad = jnp.transpose(grads, (0, 2, 1, 3, 4))
    rates = rates[:, :, :, :width].reshape(nspace, capacity, length, width, ny, nz)
    return (block_grad, jnp.transpose(rates, (3, 0, 1, 2, 4, 5))[None])


def solution(mesh):
    placed = (
        P("species", ("groups", "space"), "sub", None),
        P(("groups", "space", "sub"), "species", None, None, None),
        P("species", None, None, None, None),
        P(),
        P(("groups", "space", "sub")),
        P(("groups", "space", "sub"), None),
    )
    return jax.shard_map(
        shards,
        mesh=mesh,
        in_specs=placed,
        out_specs=(
            P(("groups", "space", "sub"), "species", None, None, None),
            P(("groups", "space", "sub"), "species", None, None, None, None, None),
        ),
        check_vma=False,
    )
```

```python
import functools
import jax
import jax.numpy as jnp
from jax import lax
from jax.experimental import pallas as pl
from jax.experimental.pallas import tpu as pltpu
from jax.sharding import PartitionSpec as P


def space_halo(fields):
    size = lax.axis_size("space")
    up = [(i, i + 1) for i in range(size - 1)]
    down = [(j, i) for i, j in up]
    before = lax.ppermute(fields[:, -1:], "space", up)
    after = lax.ppermute(fields[:, :1], "space", down)
    return before, after


def tiles_from(pieces):
    count = len(pieces)
    got = [pieces[0]]
    for d in range(1, count):
        pairs = [(j, (j - d) % count) for j in range(count)]
        got.append(lax.ppermute(pieces[d], "species", pairs))
    return got


def edges_from(edge, count):
    got = []
    for d in range(count):
        pairs = [(j * 2 + s, (j - d) % count * 2 + 1 - s) for j in range(count) for s in range(2)]
        got.append(lax.ppermute(edge, ("species", "sub"), pairs))
    return got


def rates_from(slots):
    size, me = lax.axis_size("space"), lax.axis_index("space")
    got = [lax.dynamic_index_in_dim(slots, me, 0, keepdims=False)]
    for d in range(1, size):
        piece = lax.dynamic_index_in_dim(slots, (me + d) % size, 0, keepdims=False)
        got.append(lax.ppermute(piece, "space", [(j, (j + d) % size) for j in range(size)]))
    return got


def by_sender(got):
    size, me = lax.axis_size("space"), lax.axis_index("space")
    turned = jnp.stack(got[::-1], 1)
    start = (size - 1 - me) % size
    return lax.dynamic_slice_in_dim(jnp.concatenate([turned, turned], 1), start, size, 1)


def channel_rows(value, padded):
    c, x, y, z = value.shape
    rows = jnp.transpose(value, (1, 0, 2, 3)).reshape(x, c, y * z)
    return jnp.pad(rows, ((0, 0), (0, padded - c), (0, 0)))


def packed_weight(pieces, padded):
    w = jnp.stack(pieces, 0)
    t, r, _, _, _, k = w.shape
    w = jnp.pad(w, ((0, 0), (0, padded - r), (0, 0), (0, 0), (0, 0), (0, padded - k)))
    w = jnp.transpose(w, (4, 1, 2, 3, 0, 5))
    return w.reshape(3 * padded, 9 * t * padded)


def shifted_sum(product, rows, z):
    lanes = product.shape[1]
    at = lax.broadcasted_iota(jnp.int32, (rows, lanes), 1) % z
    low = pltpu.roll(product[:rows], 1, 1)
    high = pltpu.roll(product[2 * rows :], lanes - 1, 1)
    return product[rows : 2 * rows] + jnp.where(at == 0, 0.0, low) + jnp.where(at == z - 1, 0.0, high)


def forward(count, z, ids, slot, *refs):
    mains, befores, afters = refs[:count], refs[count : 2 * count], refs[2 * count : 3 * count]
    w, wanted, misfit, slots, stack = refs[3 * count :]
    flames, length, rows, lanes = wanted.shape
    slots[...] = jnp.zeros_like(slots)
    for j in range(flames):
        first = ids[j] * length
        buf = stack.at[j % 2]
        for u in range(length):
            o = u * lanes
            for a in range(3):
                for t in range(count):
                    k = [pl.ds(((a * 3 + b) * count + t) * rows, rows) for b in range(3)]
                    main = mains[t][first + u + a]
                    buf[k[0], o : o + z] = befores[t][first + u + a]
                    buf[k[0], o + z : o + lanes] = main[:, : lanes - z]
                    buf[k[1], o : o + lanes] = main
                    buf[k[2], o : o + lanes - z] = main[:, z:]
                    buf[k[2], o + lanes - z : o + lanes] = afters[t][first + u + a]
        product = jnp.dot(w[...], buf[...], preferred_element_type=jnp.float32)
        total = shifted_sum(product, rows, z)
        place = slot[j]
        for u in range(length):
            part = total[:, u * lanes : (u + 1) * lanes]
            slots[place, u] = part.astype(slots.dtype)
            misfit[j, u] = (part - wanted[j, u].astype(jnp.float32)).astype(misfit.dtype)


def backward(count, z, *refs):
    misfits = refs[:count]
    w, grads, stack = refs[count:]
    flames, length, rows, lanes = grads.shape
    stack[...] = jnp.zeros_like(stack)
    for j in range(flames):
        buf = stack.at[j % 2]
        for u in range(length):
            o = u * lanes
            for a in range(3):
                x = u + 1 - a
                if x < 0 or x >= length:
                    continue
                for t in range(count):
                    k = [pl.ds(((a * 3 + b) * count + t) * rows, rows) for b in range(3)]
                    part = misfits[t][j, x]
                    buf[k[0], o : o + lanes - z] = part[:, z:]
                    buf[k[1], o : o + lanes] = part
                    buf[k[2], o + z : o + lanes] = part[:, : lanes - z]
        product = jnp.dot(w[...], buf[...], preferred_element_type=jnp.float32)
        total = shifted_sum(product, rows, z)
        for u in range(length):
            grads[j, u] = total[:, u * lanes : (u + 1) * lanes].astype(grads.dtype)


def shards(fields, targets, conv_weight, group_map, flame_ids, helpers):
    width = fields.shape[0]
    flames = flame_ids.shape[0]
    length, ny, nz = targets.shape[2:]
    lanes = ny * nz
    padded = -(-width // 16) * 16
    nspace = lax.axis_size("space")
    count = lax.axis_size("species")
    capacity = max(2, 2 * flames // nspace)
    tile = lax.axis_index("species")
    sub = lax.axis_index("sub")

    raw = tiles_from([fields] * count)
    raw_edges = edges_from(jnp.where(sub == 0, fields[:, :, -1], fields[:, :, 0]), count)
    halo = jnp.concatenate(space_halo(fields), 1)
    def columns(step):
        start = (tile + step) % count * width
        return lax.dynamic_slice_in_dim(conv_weight, start, width, 4)

    leaving = [columns(count - d if d else 0).reshape(width, 27 * width) for d in range(count)]
    halo, leaving = lax.optimization_barrier((halo, leaving))
    halos = tiles_from([halo] * count)
    halo_edges = edges_from(jnp.where(sub == 0, halo[:, :, -1], halo[:, :, 0]), count)
    halos, halo_edges, rows = lax.optimization_barrier((halos, halo_edges, tiles_from(leaving)))
    rows = [row.reshape(width, 3, 3, 3, width) for row in rows]

    def with_halo(inner, outer):
        return jnp.concatenate([outer[:, :1], inner, outer[:, 1:]], 1)

    mains = [channel_rows(with_halo(r, h), padded) for r, h in zip(raw, halos)]
    edges = [channel_rows(with_halo(r, h)[:, :, None], padded) for r, h in zip(raw_edges, halo_edges)]
    befores = [jnp.where(sub == 1, e, jnp.zeros_like(e)) for e in edges]
    afters = [jnp.where(sub == 0, e, jnp.zeros_like(e)) for e in edges]

    maps = [lax.dynamic_slice_in_dim(group_map, (tile + d) % count * width, width) for d in range(count)]
    same = [(maps[0][:, None] == m[None, :]).astype(jnp.bfloat16) for m in maps]
    w_fwd = packed_weight([columns(d) * same[d][:, None, None, None, :] for d in range(count)], padded)
    w_bwd = packed_weight(
        [
            jnp.transpose(jnp.flip(rows[d], 3) * same[d].T[:, None, None, None, :], (4, 1, 2, 3, 0))
            for d in range(count)
        ],
        padded,
    )

    wanted = jnp.transpose(targets, (0, 2, 1, 3, 4)).reshape(flames, length, width, lanes)
    wanted = jnp.pad(wanted, ((0, 0), (0, 0), (0, padded - width), (0, 0)))
    helper_of = helpers[:, 0]
    order = jnp.arange(flames)
    earlier = (helper_of[None, :] == helper_of[:, None]) & (order[None, :] < order[:, None])
    slot_index = helper_of * capacity + jnp.sum(earlier.astype(jnp.int32), axis=1)

    vmem = pl.BlockSpec(memory_space=pltpu.VMEM)
    smem = pl.BlockSpec(memory_space=pltpu.SMEM)
    params = pltpu.CompilerParams(vmem_limit_bytes=32 * 1024 * 1024)
    stack = pltpu.VMEM((2, 9 * count * padded, length * lanes), jnp.bfloat16)
    flops = 2 * flames * w_fwd.size * length * lanes
    cost = pl.CostEstimate(flops=flops, bytes_accessed=4_000_000, transcendentals=0)
    misfit, slots = pl.pallas_call(
        functools.partial(forward, count, nz),
        out_shape=(
            jax.ShapeDtypeStruct((flames, length, padded, lanes), jnp.bfloat16),
            jax.ShapeDtypeStruct((nspace * capacity, length, padded, lanes), jnp.bfloat16),
        ),
        in_specs=[smem, smem] + [vmem] * (3 * count + 2),
        out_specs=(vmem, vmem),
        scratch_shapes=[stack],
        compiler_params=params,
        cost_estimate=cost,
    )(flame_ids, slot_index, *mains, *befores, *afters, w_fwd, wanted)
    misfits = tiles_from([misfit] * count)
    slots = slots[:, :, :width].reshape(nspace, capacity, length, width, ny, nz)
    got = rates_from(jnp.transpose(slots, (0, 3, 1, 2, 4, 5)))
    grads = pl.pallas_call(
        functools.partial(backward, count, nz),
        out_shape=jax.ShapeDtypeStruct((flames, length, padded, lanes), jnp.bfloat16),
        in_specs=[vmem] * (count + 1),
        out_specs=vmem,
        scratch_shapes=[stack],
        compiler_params=params,
        cost_estimate=cost,
    )(*misfits, w_bwd)
    got, grads = lax.optimization_barrier((got, grads))
    grads = grads[:, :, :width].reshape(flames, length, width, ny, nz)
    return (jnp.transpose(grads, (0, 2, 1, 3, 4)), by_sender(got)[None])


def solution(mesh):
    placed = (
        P("species", ("groups", "space"), "sub", None),
        P(("groups", "space", "sub"), "species", None, None, None),
        P("species", None, None, None, None),
        P(),
        P(("groups", "space", "sub")),
        P(("groups", "space", "sub"), None),
    )
    return jax.shard_map(
        shards,
        mesh=mesh,
        in_specs=placed,
        out_specs=(
            P(("groups", "space", "sub"), "species", None, None, None),
            P(("groups", "space", "sub"), "species", None, None, None, None, None),
        ),
        check_vma=False,
    )
```

```python
import functools
import jax
import jax.numpy as jnp
from jax import lax
from jax.experimental import pallas as pl
from jax.experimental.pallas import tpu as pltpu
from jax.sharding import PartitionSpec as P


def space_halo(fields):
    size = lax.axis_size("space")
    up = [(i, i + 1) for i in range(size - 1)]
    down = [(j, i) for i, j in up]
    before = lax.ppermute(fields[:, -1:], "space", up)
    after = lax.ppermute(fields[:, :1], "space", down)
    return before, after


def tiles_from(pieces):
    count = len(pieces)
    got = [pieces[0]]
    for d in range(1, count):
        pairs = [(j, (j - d) % count) for j in range(count)]
        got.append(lax.ppermute(pieces[d], "species", pairs))
    return got


def edges_from(edge, count):
    got = []
    for d in range(count):
        pairs = [(j * 2 + s, (j - d) % count * 2 + 1 - s) for j in range(count) for s in range(2)]
        got.append(lax.ppermute(edge, ("species", "sub"), pairs))
    return got


def rates_from(slots):
    size, me = lax.axis_size("space"), lax.axis_index("space")
    got = [lax.dynamic_index_in_dim(slots, me, 0, keepdims=False)]
    for d in range(1, size):
        piece = lax.dynamic_index_in_dim(slots, (me + d) % size, 0, keepdims=False)
        got.append(lax.ppermute(piece, "space", [(j, (j + d) % size) for j in range(size)]))
    return got


def by_sender(got):
    size, me = lax.axis_size("space"), lax.axis_index("space")
    turned = jnp.stack(got[::-1], 1)
    start = (size - 1 - me) % size
    return lax.dynamic_slice_in_dim(jnp.concatenate([turned, turned], 1), start, size, 1)


def channel_rows(value, padded):
    c, x, y, z = value.shape
    rows = jnp.transpose(value, (1, 0, 2, 3)).reshape(x, c, y * z)
    return jnp.pad(rows, ((0, 0), (0, padded - c), (0, 0)))


def packed_weight(pieces, padded):
    w = jnp.stack(pieces, 0)
    t, r, _, _, _, k = w.shape
    w = jnp.pad(w, ((0, 0), (0, padded - r), (0, 0), (0, 0), (0, 0), (0, padded - k)))
    w = jnp.transpose(w, (4, 1, 2, 3, 0, 5))
    return w.reshape(3 * padded, 9 * t * padded)


def shifted_sum(pieces, z):
    first, middle, last = pieces
    rows, lanes = middle.shape
    at = lax.broadcasted_iota(jnp.int32, (rows, lanes), 1) % z
    low = pltpu.roll(first, 1, 1)
    high = pltpu.roll(last, lanes - 1, 1)
    return middle + jnp.where(at == 0, 0.0, low) + jnp.where(at == z - 1, 0.0, high)


def forward(count, z, ids, slot, *refs):
    mains, befores, afters = refs[:count], refs[count : 2 * count], refs[2 * count : 3 * count]
    w, wanted, misfit, slots, stack = refs[3 * count :]
    flames, length, rows, lanes = wanted.shape
    slots[...] = jnp.zeros_like(slots)
    for j in range(flames):
        first = ids[j] * length
        buf = stack.at[j % 2]
        for u in range(length):
            o = u * lanes
            for a in range(3):
                for t in range(count):
                    k = [pl.ds(((a * 3 + b) * count + t) * rows, rows) for b in range(3)]
                    main = mains[t][first + u + a]
                    buf[k[0], o : o + z] = befores[t][first + u + a]
                    buf[k[0], o + z : o + lanes] = main[:, : lanes - z]
                    buf[k[1], o : o + lanes] = main
                    buf[k[2], o : o + lanes - z] = main[:, z:]
                    buf[k[2], o + lanes - z : o + lanes] = afters[t][first + u + a]
        product = jnp.dot(w[...], buf[...], preferred_element_type=jnp.float32)
        total = shifted_sum([product[c * rows : (c + 1) * rows] for c in range(3)], z)
        place = slot[j]
        for u in range(length):
            part = total[:, u * lanes : (u + 1) * lanes]
            slots[place, u] = part.astype(slots.dtype)
            misfit[j, u] = (part - wanted[j, u].astype(jnp.float32)).astype(misfit.dtype)


def backward(count, z, *refs):
    misfits = refs[:count]
    w, grads, stack = refs[count:]
    flames, length, rows, lanes = grads.shape
    stack[...] = jnp.zeros_like(stack)
    for j in range(flames):
        buf = stack.at[j % 2]
        for u in range(length):
            o = u * lanes
            for a in range(3):
                x = u + 1 - a
                if x < 0 or x >= length:
                    continue
                for t in range(count):
                    k = [pl.ds(((a * 3 + b) * count + t) * rows, rows) for b in range(3)]
                    part = misfits[t][j, x]
                    buf[k[0], o : o + lanes - z] = part[:, z:]
                    buf[k[1], o : o + lanes] = part
                    buf[k[2], o + z : o + lanes] = part[:, : lanes - z]
        product = jnp.dot(w[...], buf[...], preferred_element_type=jnp.float32)
        total = shifted_sum([product[c * rows : (c + 1) * rows] for c in (2, 1, 0)], z)
        for u in range(length):
            grads[j, u] = total[:, u * lanes : (u + 1) * lanes].astype(grads.dtype)


def shards(fields, targets, conv_weight, group_map, flame_ids, helpers):
    width = fields.shape[0]
    flames = flame_ids.shape[0]
    length, ny, nz = targets.shape[2:]
    lanes = ny * nz
    padded = -(-width // 16) * 16
    nspace = lax.axis_size("space")
    count = lax.axis_size("species")
    capacity = max(2, 2 * flames // nspace)
    tile = lax.axis_index("species")
    sub = lax.axis_index("sub")

    def with_halo(inner, outer):
        return jnp.concatenate([outer[:, :1], inner, outer[:, 1:]], 1)

    raw = tiles_from([fields] * count)
    edge = jnp.where(sub == 0, fields[:, :, -1], fields[:, :, 0])
    halo = jnp.concatenate(space_halo(fields), 1)
    def columns(step):
        start = (tile + step) % count * width
        return lax.dynamic_slice_in_dim(conv_weight, start, width, 4)

    leaving = [columns(count - d if d else 0).reshape(width, 27 * width) for d in range(count)]
    halo, leaving = lax.optimization_barrier((halo, leaving))
    halos = tiles_from([halo] * count)
    halo_edge = jnp.where(sub == 0, halo[:, :, -1], halo[:, :, 0])
    edges = edges_from(with_halo(edge, halo_edge), count)
    halos, edges, rows = lax.optimization_barrier((halos, edges, tiles_from(leaving)))
    rows = [row.reshape(width, 3, 3, 3, width) for row in rows]

    mains = [channel_rows(with_halo(r, h), padded) for r, h in zip(raw, halos)]
    edges = [channel_rows(e[:, :, None], padded) for e in edges]
    befores = [jnp.where(sub == 1, e, jnp.zeros_like(e)) for e in edges]
    afters = [jnp.where(sub == 0, e, jnp.zeros_like(e)) for e in edges]

    maps = [lax.dynamic_slice_in_dim(group_map, (tile + d) % count * width, width) for d in range(count)]
    same = [(maps[0][:, None] == m[None, :]).astype(jnp.bfloat16) for m in maps]
    w_fwd = packed_weight([columns(d) * same[d][:, None, None, None, :] for d in range(count)], padded)
    w_bwd = packed_weight(
        [
            jnp.transpose(rows[d] * same[d].T[:, None, None, None, :], (4, 1, 2, 3, 0))
            for d in range(count)
        ],
        padded,
    )

    wanted = jnp.transpose(targets, (0, 2, 1, 3, 4)).reshape(flames, length, width, lanes)
    wanted = jnp.pad(wanted, ((0, 0), (0, 0), (0, padded - width), (0, 0)))
    helper_of = helpers[:, 0]
    order = jnp.arange(flames)
    earlier = (helper_of[None, :] == helper_of[:, None]) & (order[None, :] < order[:, None])
    slot_index = helper_of * capacity + jnp.sum(earlier.astype(jnp.int32), axis=1)

    vmem = pl.BlockSpec(memory_space=pltpu.VMEM)
    smem = pl.BlockSpec(memory_space=pltpu.SMEM)
    params = pltpu.CompilerParams(vmem_limit_bytes=32 * 1024 * 1024)
    stack = pltpu.VMEM((2, 9 * count * padded, length * lanes), jnp.bfloat16)
    flops = 2 * flames * w_fwd.size * length * lanes
    cost = pl.CostEstimate(flops=flops, bytes_accessed=4_000_000, transcendentals=0)
    misfit, slots = pl.pallas_call(
        functools.partial(forward, count, nz),
        out_shape=(
            jax.ShapeDtypeStruct((flames, length, padded, lanes), jnp.bfloat16),
            jax.ShapeDtypeStruct((nspace * capacity, length, padded, lanes), jnp.bfloat16),
        ),
        in_specs=[smem, smem] + [vmem] * (3 * count + 2),
        out_specs=(vmem, vmem),
        scratch_shapes=[stack],
        compiler_params=params,
        cost_estimate=cost,
    )(flame_ids, slot_index, *mains, *befores, *afters, w_fwd, wanted)
    misfits = tiles_from([misfit] * count)
    slots = slots[:, :, :width].reshape(nspace, capacity, length, width, ny, nz)
    got = rates_from(jnp.transpose(slots, (0, 3, 1, 2, 4, 5)))
    grads = pl.pallas_call(
        functools.partial(backward, count, nz),
        out_shape=jax.ShapeDtypeStruct((flames, length, padded, lanes), jnp.bfloat16),
        in_specs=[vmem] * (count + 1),
        out_specs=vmem,
        scratch_shapes=[stack],
        compiler_params=params,
        cost_estimate=cost,
    )(*misfits, w_bwd)
    grads = grads[:, :, :width].reshape(flames, length, width, ny, nz)
    block_grad = jnp.transpose(grads, (0, 2, 1, 3, 4))
    got, block_grad = lax.optimization_barrier((got, block_grad))
    return (block_grad, by_sender(got)[None])


def solution(mesh):
    placed = (
        P("species", ("groups", "space"), "sub", None),
        P(("groups", "space", "sub"), "species", None, None, None),
        P("species", None, None, None, None),
        P(),
        P(("groups", "space", "sub")),
        P(("groups", "space", "sub"), None),
    )
    return jax.shard_map(
        shards,
        mesh=mesh,
        in_specs=placed,
        out_specs=(
            P(("groups", "space", "sub"), "species", None, None, None),
            P(("groups", "space", "sub"), "species", None, None, None, None, None),
        ),
        check_vma=False,
    )
```

```python
import functools
import jax
import jax.numpy as jnp
from jax import lax
from jax.experimental import pallas as pl
from jax.experimental.pallas import tpu as pltpu
from jax.sharding import PartitionSpec as P


def space_halo(fields):
    size = lax.axis_size("space")
    up = [(i, i + 1) for i in range(size - 1)]
    down = [(j, i) for i, j in up]
    before = lax.ppermute(fields[:, -1:], "space", up)
    after = lax.ppermute(fields[:, :1], "space", down)
    return before, after


def tiles_from(pieces):
    count = len(pieces)
    got = [pieces[0]]
    for d in range(1, count):
        pairs = [(j, (j - d) % count) for j in range(count)]
        got.append(lax.ppermute(pieces[d], "species", pairs))
    return got


def edges_from(edge, count):
    got = []
    for d in range(count):
        pairs = [(j * 2 + s, (j - d) % count * 2 + 1 - s) for j in range(count) for s in range(2)]
        got.append(lax.ppermute(edge, ("species", "sub"), pairs))
    return got


def rates_from(slots):
    size, me = lax.axis_size("space"), lax.axis_index("space")
    got = [lax.dynamic_index_in_dim(slots, me, 0, keepdims=False)]
    for d in range(1, size):
        piece = lax.dynamic_index_in_dim(slots, (me + d) % size, 0, keepdims=False)
        got.append(lax.ppermute(piece, "space", [(j, (j + d) % size) for j in range(size)]))
    return got


def by_sender(got):
    size, me = lax.axis_size("space"), lax.axis_index("space")
    turned = jnp.stack(got[::-1], 1)
    start = (size - 1 - me) % size
    return lax.dynamic_slice_in_dim(jnp.concatenate([turned, turned], 1), start, size, 1)


def channel_rows(value, padded):
    c, x, y, z = value.shape
    rows = jnp.transpose(value, (1, 0, 2, 3)).reshape(x, c, y * z)
    return jnp.pad(rows, ((0, 0), (0, padded - c), (0, 0)))


def packed_weight(pieces, padded):
    w = jnp.stack(pieces, 0)
    t, r, _, _, _, k = w.shape
    w = jnp.pad(w, ((0, 0), (0, padded - r), (0, 0), (0, 0), (0, 0), (0, padded - k)))
    w = jnp.transpose(w, (4, 1, 2, 3, 0, 5))
    return w.reshape(3 * padded, 9 * t * padded)


def shifted_sum(pieces, z):
    first, middle, last = pieces
    rows, lanes = middle.shape
    at = lax.broadcasted_iota(jnp.int32, (rows, lanes), 1) % z
    low = pltpu.roll(first, 1, 1)
    high = pltpu.roll(last, lanes - 1, 1)
    return middle + jnp.where(at == 0, 0.0, low) + jnp.where(at == z - 1, 0.0, high)


def forward(count, z, ids, slot, *refs):
    mains, befores, afters = refs[:count], refs[count : 2 * count], refs[2 * count : 3 * count]
    w, wanted, misfit, slots, stack = refs[3 * count :]
    flames, length, rows, lanes = wanted.shape
    slots[...] = jnp.zeros_like(slots)
    for j in range(flames):
        first = ids[j] * length
        buf = stack.at[j % 2]
        for u in range(length):
            o = u * lanes
            for a in range(3):
                for t in range(count):
                    k = [pl.ds(((a * 3 + b) * count + t) * rows, rows) for b in range(3)]
                    main = mains[t][first + u + a]
                    buf[k[0], o : o + z] = befores[t][first + u + a]
                    buf[k[0], o + z : o + lanes] = main[:, : lanes - z]
                    buf[k[1], o : o + lanes] = main
                    buf[k[2], o : o + lanes - z] = main[:, z:]
                    buf[k[2], o + lanes - z : o + lanes] = afters[t][first + u + a]
        product = jnp.dot(w[...], buf[...], preferred_element_type=jnp.float32)
        total = shifted_sum([product[c * rows : (c + 1) * rows] for c in range(3)], z)
        place = slot[j]
        for u in range(length):
            part = total[:, u * lanes : (u + 1) * lanes]
            slots[place, u] = part.astype(slots.dtype)
            misfit[j, u] = (part - wanted[j, u].astype(jnp.float32)).astype(misfit.dtype)


def backward(count, z, *refs):
    misfits = refs[:count]
    w, grads, stack = refs[count:]
    flames, length, rows, lanes = grads.shape
    stack[...] = jnp.zeros_like(stack)
    for j in range(flames):
        buf = stack.at[j % 2]
        for u in range(length):
            o = u * lanes
            for a in range(3):
                x = u + 1 - a
                if x < 0 or x >= length:
                    continue
                for t in range(count):
                    k = [pl.ds(((a * 3 + b) * count + t) * rows, rows) for b in range(3)]
                    part = misfits[t][j, x]
                    buf[k[0], o : o + lanes - z] = part[:, z:]
                    buf[k[1], o : o + lanes] = part
                    buf[k[2], o + z : o + lanes] = part[:, : lanes - z]
        product = jnp.dot(w[...], buf[...], preferred_element_type=jnp.float32)
        total = shifted_sum([product[c * rows : (c + 1) * rows] for c in (2, 1, 0)], z)
        for u in range(length):
            grads[j, u] = total[:, u * lanes : (u + 1) * lanes].astype(grads.dtype)


def shards(fields, targets, conv_weight, group_map, flame_ids, helpers):
    width = fields.shape[0]
    flames = flame_ids.shape[0]
    length, ny, nz = targets.shape[2:]
    lanes = ny * nz
    padded = -(-width // 16) * 16
    nspace = lax.axis_size("space")
    count = lax.axis_size("species")
    capacity = max(2, 2 * flames // nspace)
    tile = lax.axis_index("species")
    sub = lax.axis_index("sub")

    def with_halo(inner, outer):
        return jnp.concatenate([outer[:, :1], inner, outer[:, 1:]], 1)

    raw = tiles_from([fields] * count)
    edge = jnp.where(sub == 0, fields[:, :, -1], fields[:, :, 0])
    halo = jnp.concatenate(space_halo(fields), 1)
    def columns(step):
        start = (tile + step) % count * width
        return lax.dynamic_slice_in_dim(conv_weight, start, width, 4)

    leaving = [columns(count - d if d else 0).reshape(width, 27 * width) for d in range(count)]
    raw_edges = edges_from(edge, count)
    rows = tiles_from(leaving)
    halo, raw_edges, rows = lax.optimization_barrier((halo, raw_edges, rows))
    halos = tiles_from([halo] * count)
    halo_edges = edges_from(jnp.where(sub == 0, halo[:, :, -1], halo[:, :, 0]), count)
    edges = [with_halo(e, h) for e, h in zip(raw_edges, halo_edges)]
    rows = [row.reshape(width, 3, 3, 3, width) for row in rows]

    mains = [channel_rows(with_halo(r, h), padded) for r, h in zip(raw, halos)]
    edges = [channel_rows(e[:, :, None], padded) for e in edges]
    befores = [jnp.where(sub == 1, e, jnp.zeros_like(e)) for e in edges]
    afters = [jnp.where(sub == 0, e, jnp.zeros_like(e)) for e in edges]

    maps = [lax.dynamic_slice_in_dim(group_map, (tile + d) % count * width, width) for d in range(count)]
    same = [(maps[0][:, None] == m[None, :]).astype(jnp.bfloat16) for m in maps]
    w_fwd = packed_weight([columns(d) * same[d][:, None, None, None, :] for d in range(count)], padded)
    w_bwd = packed_weight(
        [
            jnp.transpose(rows[d] * same[d].T[:, None, None, None, :], (4, 1, 2, 3, 0))
            for d in range(count)
        ],
        padded,
    )

    wanted = jnp.transpose(targets, (0, 2, 1, 3, 4)).reshape(flames, length, width, lanes)
    wanted = jnp.pad(wanted, ((0, 0), (0, 0), (0, padded - width), (0, 0)))
    helper_of = helpers[:, 0]
    order = jnp.arange(flames)
    earlier = (helper_of[None, :] == helper_of[:, None]) & (order[None, :] < order[:, None])
    slot_index = helper_of * capacity + jnp.sum(earlier.astype(jnp.int32), axis=1)

    vmem = pl.BlockSpec(memory_space=pltpu.VMEM)
    smem = pl.BlockSpec(memory_space=pltpu.SMEM)
    params = pltpu.CompilerParams(vmem_limit_bytes=32 * 1024 * 1024)
    stack = pltpu.VMEM((2, 9 * count * padded, length * lanes), jnp.bfloat16)
    flops = 2 * flames * w_fwd.size * length * lanes
    cost = pl.CostEstimate(flops=flops, bytes_accessed=4_000_000, transcendentals=0)
    misfit, slots = pl.pallas_call(
        functools.partial(forward, count, nz),
        out_shape=(
            jax.ShapeDtypeStruct((flames, length, padded, lanes), jnp.bfloat16),
            jax.ShapeDtypeStruct((nspace * capacity, length, padded, lanes), jnp.bfloat16),
        ),
        in_specs=[smem, smem] + [vmem] * (3 * count + 2),
        out_specs=(vmem, vmem),
        scratch_shapes=[stack],
        compiler_params=params,
        cost_estimate=cost,
    )(flame_ids, slot_index, *mains, *befores, *afters, w_fwd, wanted)
    misfits = tiles_from([misfit] * count)
    slots = slots[:, :, :width].reshape(nspace, capacity, length, width, ny, nz)
    got = rates_from(jnp.transpose(slots, (0, 3, 1, 2, 4, 5)))
    grads = pl.pallas_call(
        functools.partial(backward, count, nz),
        out_shape=jax.ShapeDtypeStruct((flames, length, padded, lanes), jnp.bfloat16),
        in_specs=[vmem] * (count + 1),
        out_specs=vmem,
        scratch_shapes=[stack],
        compiler_params=params,
        cost_estimate=cost,
    )(*misfits, w_bwd)
    grads = grads[:, :, :width].reshape(flames, length, width, ny, nz)
    block_grad = jnp.transpose(grads, (0, 2, 1, 3, 4))
    got, block_grad = lax.optimization_barrier((got, block_grad))
    return (block_grad, by_sender(got)[None])


def solution(mesh):
    placed = (
        P("species", ("groups", "space"), "sub", None),
        P(("groups", "space", "sub"), "species", None, None, None),
        P("species", None, None, None, None),
        P(),
        P(("groups", "space", "sub")),
        P(("groups", "space", "sub"), None),
    )
    return jax.shard_map(
        shards,
        mesh=mesh,
        in_specs=placed,
        out_specs=(
            P(("groups", "space", "sub"), "species", None, None, None),
            P(("groups", "space", "sub"), "species", None, None, None, None, None),
        ),
        check_vma=False,
    )
```
